128 devices in a mesh: dp: 8 (over x, z_hi), seq: 16 (over y, z_lo, core).
Axes of the slice: x: 4, y: 4, z: 4 (z_hi: 2, z_lo: 2; z = z_hi * 2 + z_lo), core: 2. Of those that a mesh axis runs over, the one named last changes fastest.
Arguments:
- spatial_queries: bfloat16 [8, 16, 400, 3072], P('dp', 'seq'), may hold values from -180 to 180
- spatial_keys: bfloat16 [8, 16, 400, 3072], P('dp', 'seq'), may hold values from -7 to 7
- spatial_values: bfloat16 [8, 16, 400, 3072], P('dp', 'seq'), may hold values from -6 to 6
- spatial_cotangent: bfloat16 [8, 16, 400, 3072], P('dp', 'seq'), may hold values from -54 to 54
- temporal_queries: bfloat16 [8, 16, 400, 1536], P('dp', 'seq'), may hold values from -180 to 180
- temporal_keys: bfloat16 [8, 16, 400, 1536], P('dp', 'seq'), may hold values from -7 to 7
- temporal_values: bfloat16 [8, 16, 400, 1536], P('dp', 'seq'), may hold values from -6 to 6
- temporal_cotangent: bfloat16 [8, 16, 400, 1536], P('dp', 'seq'), may hold values from -54 to 54
- frame_bias: float32 [12, 31], replicated, may hold values from -4 to 4
- frame_count: int32 [8], P('dp'), may hold values from 8 to 16, as said below
- grid_height: int32 [8], P('dp'), may hold values from 10 to 20, as said below
- grid_width: int32 [8], P('dp'), may hold values from 10 to 20, as said below
Outputs:
- spatial_query_grad: bfloat16 [8, 16, 400, 3072], P('dp', 'seq')
- spatial_key_grad: bfloat16 [8, 16, 400, 3072], P('dp', 'seq')
- spatial_value_grad: bfloat16 [8, 16, 400, 3072], P('dp', 'seq')
- temporal_query_grad: bfloat16 [8, 16, 400, 1536], P('dp', 'seq')
- temporal_key_grad: bfloat16 [8, 16, 400, 1536], P('dp', 'seq')
- temporal_value_grad: bfloat16 [8, 16, 400, 1536], P('dp', 'seq')
- table_grad: float32 [12, 31], replicated
The draws below stay inside these ranges and needn't reach their ends.
Inputs may be any that keep to these rules, and one draw needn't show every extreme that they name: `frame_count`: some clip has 16 frames. `grid_height`: some clip has 20 patch rows. `grid_width`: some clip has 20 patch columns.
All inputs are finite; a program needn't handle non-finite values.
Results may differ from the reference program's by a relative error of at most 0.0074.
Values may be sent and summed in bfloat16 or wider, within the bound.
A program may use at most 128 MiB of HBM per device.

```python
import math
import jax
import jax.numpy as jnp
from jax import lax

HEAD = 128
SP_HEADS = 24
TM_HEADS = 12
D_SP = 3072
D_TM = 1536
GRID = 20
PATCH = 400
FRAMES = 16
CLIPS = 8


def base_field(key, width):
    return jax.random.truncated_normal(key, -6.0, 6.0, (CLIPS, FRAMES, PATCH, width), jnp.float32)


def spatial_base(key):
    return base_field(jax.random.fold_in(key, 100), SP_HEADS * HEAD)


def temporal_base(key):
    return base_field(jax.random.fold_in(key, 200), TM_HEADS * HEAD)


def draw_spatial_queries(key, part):
    key = jax.random.fold_in(key, 1)
    drawn = base_field(key, SP_HEADS * HEAD)
    return drawn.astype(jnp.bfloat16)


def draw_spatial_keys(key, part):
    base = spatial_base(key)
    return base.astype(jnp.bfloat16)


def draw_temporal_queries(key, part):
    key = jax.random.fold_in(key, 8)
    drawn = base_field(key, TM_HEADS * HEAD)
    return drawn.astype(jnp.bfloat16)


def draw_temporal_keys(key, part):
    base = temporal_base(key)
    return base.astype(jnp.bfloat16)


def cotangent_parts(key):
    first_key, second_key = jax.random.split(key, 2)
    ramp_pos = (jnp.arange(CLIPS)[:, None] * PATCH + jnp.arange(PATCH)[None, :]).astype(jnp.float32) / (CLIPS * PATCH)
    ramp = (0.3 * 3.0 ** ramp_pos)[:, None, :, None]
    spread = 10.0 ** jax.random.uniform(second_key, (CLIPS, FRAMES, PATCH, 1), jnp.float32)
    return (first_key, ramp * spread)


def draw_spatial_cotangent(key, part):
    key = jax.random.fold_in(key, 3)
    first_key, scale = cotangent_parts(key)
    return (scale * base_field(first_key, SP_HEADS * HEAD)).astype(jnp.bfloat16)


def draw_temporal_cotangent(key, part):
    key = jax.random.fold_in(key, 7)
    first_key, scale = cotangent_parts(key)
    return (scale * base_field(first_key, TM_HEADS * HEAD)).astype(jnp.bfloat16)


def capped_draw(key, lowest, highest):
    first_key, second_key = jax.random.split(key)
    counts = jax.random.randint(first_key, (CLIPS,), lowest, highest + 1, jnp.int32)
    chosen = jax.random.randint(second_key, (), 0, CLIPS, jnp.int32)
    return jnp.where(jnp.arange(CLIPS, dtype=jnp.int32) == chosen, highest, counts).astype(jnp.int32)


def draw_frame_count(key, part):
    key = jax.random.fold_in(key, 4)
    return capped_draw(key, FRAMES // 2, FRAMES)


def draw_grid_height(key, part):
    key = jax.random.fold_in(key, 5)
    return capped_draw(key, GRID // 2, GRID)


def draw_grid_width(key, part):
    key = jax.random.fold_in(key, 6)
    return capped_draw(key, GRID // 2, GRID)


def levels(rng, extent, pieces, least, largest):
    loudness, own = 1.0, jax.random.fold_in(rng, 6)
    for dim, blocks in pieces:
        draws = jnp.exp(jax.random.uniform(jax.random.fold_in(own, dim), (blocks,), jnp.float32, least / len(pieces), largest / len(pieces)))
        loudness = loudness * jnp.repeat(draws, extent[dim] // blocks).reshape([-1 if axis == dim else 1 for axis in range(len(extent))])
    return loudness


def scatter_about(rng, extent, scale, reach, shards=(), kind=jnp.bfloat16):
    drawn = jax.random.normal(rng, extent, jnp.float32) * scale
    if len(shards) > 0:
        drawn = levels(rng, extent, shards, -0.22, 0.18) * drawn
    return jnp.clip(drawn, min=-reach, max=reach).astype(kind)


def setup_inputs(seed: int = 0) -> dict:
    arg_keys = jax.random.split(jax.random.key(seed), 13)
    spatial_queries = draw_spatial_queries(jax.random.fold_in(arg_keys[12], 71), 0)
    spatial_keys = draw_spatial_keys(jax.random.fold_in(arg_keys[12], 71), 0)
    spatial_values = scatter_about(arg_keys[2], (CLIPS, FRAMES, PATCH, D_SP), 1.0, 6.0, ((0, 8), (1, 16)))
    spatial_cotangent = draw_spatial_cotangent(jax.random.fold_in(arg_keys[12], 71), 0)
    temporal_queries = draw_temporal_queries(jax.random.fold_in(arg_keys[12], 71), 0)
    temporal_keys = draw_temporal_keys(jax.random.fold_in(arg_keys[12], 71), 0)
    temporal_values = scatter_about(arg_keys[6], (CLIPS, FRAMES, PATCH, D_TM), 1.0, 6.0, ((0, 8), (1, 16)))
    temporal_cotangent = draw_temporal_cotangent(jax.random.fold_in(arg_keys[12], 71), 0)
    frame_bias = scatter_about(arg_keys[8], (TM_HEADS, 2 * FRAMES - 1), 1.0, 4.0, (), jnp.float32)
    frame_count = draw_frame_count(jax.random.fold_in(arg_keys[12], 71), 0)
    grid_height = draw_grid_height(jax.random.fold_in(arg_keys[12], 71), 0)
    grid_width = draw_grid_width(jax.random.fold_in(arg_keys[12], 71), 0)
    return dict(spatial_queries=spatial_queries, spatial_keys=spatial_keys, spatial_values=spatial_values, spatial_cotangent=spatial_cotangent, temporal_queries=temporal_queries, temporal_keys=temporal_keys, temporal_values=temporal_values, temporal_cotangent=temporal_cotangent, frame_bias=frame_bias, frame_count=frame_count, grid_height=grid_height, grid_width=grid_width)


def attend(queries_in, keys_in, values_in, upstream, bias_term, live_rows, live_keys):
    scaling = 1.0 / math.sqrt(queries_in.shape[-1])
    high = lax.Precision.HIGHEST
    query_wide = queries_in.astype(jnp.float32)
    key_wide = keys_in.astype(jnp.float32)
    value_wide = values_in.astype(jnp.float32)
    upstream_wide = upstream.astype(jnp.float32)
    scores = jnp.einsum('bqhe,bkhe->bhqk', query_wide, key_wide, precision=high) * scaling + bias_term
    keep_key = live_keys[:, None, None, :]
    scores = jnp.where(keep_key, scores, -1e+30)
    highest = lax.optimization_barrier(jnp.max(scores, axis=-1, keepdims=True))
    weights = jnp.where(keep_key, jnp.exp(scores - highest), 0.0)
    live_row = live_rows[:, None, :, None]
    totals = jnp.where(live_row, lax.optimization_barrier(jnp.sum(weights, axis=-1, keepdims=True)), 1.0)
    attention = jnp.where(live_row, weights / totals, 0.0)
    attention_low = lax.optimization_barrier(attention.astype(jnp.bfloat16)).astype(jnp.float32)
    result = jnp.einsum('bhqk,bkhe->bqhe', attention_low, value_wide, precision=high)
    grad_attention = jnp.einsum('bqhe,bkhe->bhqk', upstream_wide, value_wide, precision=high)
    row_delta = jnp.einsum('bqhe,bqhe->bhq', upstream_wide, result, precision=high)[..., None]
    grad_score = attention * (grad_attention - row_delta)
    grad_low = lax.optimization_barrier(grad_score.astype(jnp.bfloat16)).astype(jnp.float32)
    grad_query = (jnp.einsum('bhqk,bkhe->bqhe', grad_low, key_wide, precision=high) * scaling).astype(jnp.bfloat16)
    grad_keys = (jnp.einsum('bhqk,bqhe->bkhe', grad_low, query_wide, precision=high) * scaling).astype(jnp.bfloat16)
    grad_values = jnp.einsum('bhqk,bqhe->bkhe', attention_low, upstream_wide, precision=high).astype(jnp.bfloat16)
    return (grad_query, grad_keys, grad_values, lax.optimization_barrier(jnp.sum(grad_score, axis=0)))

def live_mask(frame_count, grid_height, grid_width):
    frame_ids = jnp.arange(FRAMES, dtype=jnp.int32)
    patch_ids = jnp.arange(PATCH, dtype=jnp.int32)
    in_frames = frame_ids[None, :, None] < frame_count[:, None, None]
    in_rows = (patch_ids // GRID)[None, None, :] < grid_height[:, None, None]
    in_columns = (patch_ids % GRID)[None, None, :] < grid_width[:, None, None]
    return in_frames & in_rows & in_columns

def reference(spatial_queries, spatial_keys, spatial_values, spatial_cotangent, temporal_queries, temporal_keys, temporal_values, temporal_cotangent, frame_bias, frame_count, grid_height, grid_width):
    live = live_mask(frame_count, grid_height, grid_width)
    spatial_arrays = (spatial_queries, spatial_keys, spatial_values, spatial_cotangent)
    temporal_arrays = (temporal_queries, temporal_keys, temporal_values, temporal_cotangent)

    def spatial_one(items):
        grads = attend(items[0][None], items[1][None], items[2][None], items[3][None], 0.0, items[4][None], items[4][None])
        return (grads[0][0], grads[1][0], grads[2][0])
    spatial_pieces = tuple((a.reshape(CLIPS * FRAMES, PATCH, SP_HEADS, HEAD) for a in spatial_arrays))
    spatial_grads = lax.map(spatial_one, spatial_pieces + (live.reshape(CLIPS * FRAMES, PATCH),))
    spatial_grads = tuple((g.reshape(CLIPS, FRAMES, PATCH, SP_HEADS * HEAD) for g in spatial_grads))
    offsets = jnp.arange(FRAMES, dtype=jnp.int32)[None, :] - jnp.arange(FRAMES, dtype=jnp.int32)[:, None] + FRAMES - 1
    bias_term = frame_bias[:, offsets]

    def temporal_one(items):
        return attend(items[0], items[1], items[2], items[3], bias_term, items[4], items[4])
    temporal_pieces = tuple((jnp.transpose(a.reshape(CLIPS, FRAMES, PATCH, TM_HEADS, HEAD), (0, 2, 1, 3, 4)) for a in temporal_arrays))
    grad_query, grad_keys, grad_values, grad_score = lax.map(temporal_one, temporal_pieces + (jnp.transpose(live, (0, 2, 1)),))
    temporal_grads = tuple((jnp.transpose(g, (0, 2, 1, 3, 4)).reshape(CLIPS, FRAMES, PATCH, TM_HEADS * HEAD) for g in (grad_query, grad_keys, grad_values)))
    selector = (offsets[:, :, None] == jnp.arange(2 * FRAMES - 1, dtype=jnp.int32)[None, None, :]).astype(jnp.float32)
    table_grad = jnp.einsum('hij,ijd->hd', lax.optimization_barrier(jnp.sum(grad_score, axis=0)), selector, precision=lax.Precision.HIGHEST)
    return (spatial_grads[0], spatial_grads[1], spatial_grads[2], temporal_grads[0], temporal_grads[1], temporal_grads[2], table_grad)
```

```python
import functools
import math

import jax
import jax.numpy as jnp
from jax import lax
from jax.experimental import pallas as pl
from jax.experimental.pallas import tpu as pltpu
from jax.sharding import PartitionSpec as P

MESH = pl.DeviceIdType.MESH
HEAD = 128
GRID = 20
PATCH = 400
ROWS = 16
TILES = PATCH // ROWS
FRAMES = 16
DP = 8
SP_HEADS = 24
TM_HEADS = 12
SLOTS = 19
CHUNKS = ((0, 6), (6, 6), (12, 7))
GROUP = 3
GROUPS = SP_HEADS // GROUP
QPAD = 512
SCALE = 1.0 / math.sqrt(HEAD)
LOG2E = math.log2(math.e)
DEAD = -1e30
F32 = jnp.float32
BF16 = jnp.bfloat16

STEPS = (
    (2, 1, 0), (1, 0, 0), (3, 1, 0), (2, 0, 0), (1, 1, 0), (3, 0, 0), (0, 1, 0),
    (2, 0, 1), (2, 1, 1), (1, 0, 1), (3, 1, 1), (0, 0, 1), (1, 1, 1), (3, 0, 1), (0, 1, 1),
)


def dot(a, b, dims):
    return lax.dot_general(a, b, (dims, ((), ())), preferred_element_type=F32)


def attend(q, k, v, g, key_bias, query_live):
    scores = dot(k, q, ((1,), (1,))) * (SCALE * LOG2E) + key_bias
    weights = jnp.exp2(scores - jnp.max(scores, axis=0, keepdims=True))
    attention = weights * (query_live / jnp.sum(weights, axis=0, keepdims=True))
    low = attention.astype(BF16)
    grad_attention = dot(v, g, ((1,), (1,)))
    delta = jnp.sum(low.astype(F32) * grad_attention, axis=0, keepdims=True)
    grad_score = attention * (grad_attention - delta)
    grad_low = grad_score.astype(BF16)
    grad_value = dot(low, g, ((1,), (0,)))
    grad_key = dot(grad_low, q, ((1,), (0,))) * SCALE
    grad_query = dot(k, grad_low, ((0,), (0,))).T * SCALE
    return grad_query.astype(BF16), grad_key.astype(BF16), grad_value.astype(BF16), grad_score


def kernel(
    sq, sk, sv, sg, tq, tk, tv, tg, bias, count, height, width,
    osq, osk, osv, otq, otk, otv, table,
    held, made, recv, back, bias_mat, score_sum, bins, parts, sums,
    load_sem, store_sem, out_sem, in_sem, own_sem, home_sem, home_recv, home_own,
    dp_send, dp_recv, sum_send, sum_recv,
):
    me = lax.axis_index("seq")
    my_dp = lax.axis_index("dp")
    y, z, core = me // 4, (me // 2) % 2, me % 2
    spatial_in, spatial_out = (sq, sk, sv, sg), (osq, osk, osv)
    temporal_in, temporal_out = (tq, tk, tv, tg), (otq, otk, otv)

    def peer(step):
        return ((y + step[0]) % 4) * 4 + ((z + step[1]) % 2) * 2 + (core + step[2]) % 2

    def slot_of(step):
        return step[0] * 4 + step[1] * 2 + step[2]

    def unit_of(device, first):
        r = device % 4
        unit = SLOTS * r + first
        if first >= 12:
            unit = unit - r // 3
        return 3 * (device // 4) + unit // TILES, unit % TILES

    def tile_rows(tile, n):
        return pl.ds(pl.multiple_of(tile * ROWS, ROWS), n * ROWS)

    def head_cols(head):
        return pl.ds(pl.multiple_of(head * HEAD, HEAD), HEAD)

    barrier = pltpu.get_barrier_semaphore()
    for step in STEPS:
        pl.semaphore_signal(barrier, inc=1, device_id={"seq": peer(step)}, device_id_type=MESH)
    for i in range(1, DP):
        pl.semaphore_signal(
            barrier, inc=1, device_id={"dp": (my_dp + i) % DP}, device_id_type=MESH
        )

    def load(group, a):
        cols = pl.ds(pl.multiple_of(group * GROUP * HEAD, HEAD), GROUP * HEAD)
        return pltpu.make_async_copy(
            spatial_in[a].at[:, cols], held.at[a, pl.ds(0, PATCH), cols], load_sem.at[group]
        )

    @pl.loop(0, GROUPS)
    def _(group):
        for a in range(4):
            load(group, a).start()

    for c, (first, n) in enumerate(CHUNKS):
        head, tile = unit_of(me, first)
        for a in range(4):
            pltpu.make_async_copy(
                temporal_in[a].at[tile_rows(tile, n), head_cols(head)],
                recv.at[a, 0, pl.ds(first * ROWS, n * ROWS)],
                own_sem.at[c],
            ).start()

    pl.semaphore_wait(barrier, len(STEPS) + DP - 1)

    for c, (first, n) in enumerate(CHUNKS):
        for step in STEPS:
            to = peer(step)
            head, tile = unit_of(to, first)
            for a in range(4):
                pltpu.make_async_remote_copy(
                    src_ref=temporal_in[a].at[tile_rows(tile, n), head_cols(head)],
                    dst_ref=recv.at[a, slot_of(step), pl.ds(first * ROWS, n * ROWS)],
                    send_sem=out_sem.at[0],
                    recv_sem=in_sem.at[c],
                    device_id={"seq": to},
                    device_id_type=MESH,
                ).start()

    def inside(patch):
        row = (patch * 3277) >> 16
        return ((row < height[0]) & (patch - row * GRID < width[0])).astype(F32)

    def frame_of(slot):
        dy, dz, dc = slot >> 2, (slot >> 1) & 1, slot & 1
        return ((y - dy) & 3) * 4 + ((z + dz) & 1) * 2 + ((core + dc) & 1)

    alive = (me < count[0]).astype(F32)
    key_live = inside(lax.broadcasted_iota(jnp.int32, (PATCH, 1), 0)) * alive
    key_bias = (1.0 - key_live) * DEAD
    queries = lax.broadcasted_iota(jnp.int32, (1, QPAD), 1)
    query_live = inside(queries) * alive * (queries < PATCH).astype(F32)

    held[0, pl.ds(PATCH, QPAD - PATCH), :] = jnp.zeros((QPAD - PATCH, SP_HEADS * HEAD), BF16)
    held[3, pl.ds(PATCH, QPAD - PATCH), :] = jnp.zeros((QPAD - PATCH, SP_HEADS * HEAD), BF16)
    bins[...] = jnp.zeros_like(bins)
    parts[my_dp] = jnp.zeros(parts.shape[1:], F32)

    def spatial(start, stop):
        @pl.loop(start, stop)
        def _(group):
            cols = pl.ds(pl.multiple_of(group * GROUP * HEAD, HEAD), GROUP * HEAD)
            arrived = held.at[:, pl.ds(0, PATCH), cols]
            pltpu.make_async_copy(arrived, arrived, load_sem.at[group]).wait()

            @pl.loop(0, GROUP)
            def _(j):
                own = head_cols(group * GROUP + j)
                grads = attend(
                    held[0, :, own],
                    held[1, pl.ds(0, PATCH), own],
                    held[2, pl.ds(0, PATCH), own],
                    held[3, :, own],
                    key_bias,
                    query_live,
                )
                made[0, :, own] = grads[0][:PATCH]
                made[1, :, own] = grads[1]
                made[2, :, own] = grads[2]

            for a in range(3):
                pltpu.make_async_copy(
                    made.at[a, :, cols], spatial_out[a].at[:, cols], store_sem.at[0]
                ).start()

    def temporal(c):
        first, n = CHUNKS[c]
        head, tile = unit_of(me, first)
        side = FRAMES * ROWS
        key_at = lax.broadcasted_iota(jnp.int32, (side, 1), 0)
        query_at = lax.broadcasted_iota(jnp.int32, (1, side), 1)
        key_frame, query_frame = frame_of(key_at >> 4), frame_of(query_at >> 4)
        same = (key_at & 15) == (query_at & 15)
        apart = jnp.where(same, key_frame - query_frame + (FRAMES - 1), -1)
        frame_dead = jnp.where(key_frame < count[0], 0.0, DEAD)
        bias_mat[...] = jnp.where(same, frame_dead, DEAD)

        @pl.loop(0, 2 * FRAMES - 1)
        def _(d):
            bias_mat[...] += jnp.where(apart == d, bias[head, d] * LOG2E, 0.0)

        score_sum[...] = jnp.zeros_like(score_sum)

        own, arrived = recv.at[:, 0], recv.at[:, pl.ds(1, FRAMES - 1)]
        rows = pl.ds(first * ROWS, n * ROWS)
        own, arrived = own.at[:, rows], arrived.at[:, :, rows]
        pltpu.make_async_copy(own, own, own_sem.at[c]).wait()
        pltpu.make_async_copy(arrived, arrived, in_sem.at[c]).wait()

        @pl.loop(0, n)
        def _(i):
            slot_rows = pl.ds(pl.multiple_of((first + i) * ROWS, ROWS), ROWS)
            patch = (tile + i) * ROWS + (query_at & 15)
            live = inside(patch) * (query_frame < count[0]).astype(F32)
            if first >= 12:
                live = live * (1 - (me % 4) // 3 * (i < 1).astype(jnp.int32)).astype(F32)
            q, k, v, g = (
                recv[a, :, slot_rows, :].reshape(side, HEAD) for a in range(4)
            )
            grads = attend(q, k, v, g, bias_mat[...], live)
            score_sum[...] += grads[3]
            for a in range(3):
                back[a, :, slot_rows, :] = grads[a].reshape(FRAMES, ROWS, HEAD)

        folded = jnp.sum(score_sum[...].reshape(FRAMES, ROWS, side), axis=1)
        slots = lax.broadcasted_iota(jnp.int32, (FRAMES, 1), 0)
        distance = frame_of(slots) - query_frame + (FRAMES - 1)

        @pl.loop(0, 2 * FRAMES - 1)
        def _(d):
            bins[pl.ds(d, 1), :] = jnp.sum(
                jnp.where(distance == d, folded, 0.0), axis=0, keepdims=True
            )

        column = jnp.sum(bins[...], axis=1, keepdims=True)
        lanes = lax.broadcasted_iota(jnp.int32, (1, HEAD), 1)
        parts[my_dp] += jnp.where(lanes == head, column, 0.0)

    def home(c):
        first, n = CHUNKS[c]
        head, tile = unit_of(me, first)
        pieces = [(first, 6, tile)]
        if n == 7:
            spare = (me % 4) // 3
            pieces = [(first + 1, 6, tile + 1), (first, 1, tile * (1 - spare) + TILES * spare)]
        for slot, size, at in pieces:
            rows = pl.ds(slot * ROWS, size * ROWS)
            for a in range(3):
                pltpu.make_async_copy(
                    back.at[a, 0, rows],
                    temporal_out[a].at[tile_rows(at, size), head_cols(head)],
                    home_own.at[0],
                ).start()
            for step in STEPS:
                from_slot = ((4 - step[0]) % 4) * 4 + step[1] * 2 + step[2]
                for a in range(3):
                    pltpu.make_async_remote_copy(
                        src_ref=back.at[a, from_slot, rows],
                        dst_ref=temporal_out[a].at[tile_rows(at, size), head_cols(head)],
                        send_sem=home_sem.at[0],
                        recv_sem=home_recv.at[0],
                        device_id={"seq": peer(step)},
                        device_id_type=MESH,
                    ).start()

    spatial(0, 4)
    temporal(0)
    home(0)
    spatial(4, GROUPS)
    temporal(1)
    home(1)
    temporal(2)

    dp_copies = [
        pltpu.make_async_remote_copy(
            src_ref=parts.at[my_dp],
            dst_ref=parts.at[my_dp],
            send_sem=dp_send.at[0],
            recv_sem=dp_recv.at[0],
            device_id={"dp": (my_dp + i) % DP},
            device_id_type=MESH,
        )
        for i in range(1, DP)
    ]
    for copy in dp_copies:
        copy.start()
    home(2)
    seven = parts.at[pl.ds(0, DP - 1)]
    pltpu.make_async_copy(seven, seven, dp_recv.at[0]).wait()
    pltpu.make_async_copy(seven, seven, dp_send.at[0]).wait()
    sums[0] = functools.reduce(jnp.add, [parts[i] for i in range(DP)])
    for step in STEPS:
        pltpu.make_async_remote_copy(
            src_ref=sums.at[0],
            dst_ref=sums.at[slot_of(step)],
            send_sem=sum_send.at[0],
            recv_sem=sum_recv.at[0],
            device_id={"seq": peer(step)},
            device_id_type=MESH,
        ).start()
    others = sums.at[pl.ds(1, FRAMES - 1)]
    pltpu.make_async_copy(others, others, sum_recv.at[0]).wait()
    pltpu.make_async_copy(others, others, sum_send.at[0]).wait()
    total = functools.reduce(jnp.add, [sums[i] for i in range(FRAMES)])
    wide = jnp.concatenate([total, jnp.zeros((HEAD - total.shape[0], HEAD), F32)], axis=0)
    table[...] = wide.T[:TM_HEADS, : 2 * FRAMES - 1]

    pltpu.make_async_copy(made, made, store_sem.at[0]).wait()
    sent = recv.at[:, pl.ds(1, FRAMES - 1)]
    pltpu.make_async_copy(sent, sent, out_sem.at[0]).wait()
    own, others = back.at[:, 0], back.at[:, pl.ds(1, FRAMES - 1)]
    pltpu.make_async_copy(own, own, home_own.at[0]).wait()
    pltpu.make_async_copy(others, others, home_sem.at[0]).wait()
    pltpu.make_async_copy(others, others, home_recv.at[0]).wait()


def per_device(
    spatial_queries,
    spatial_keys,
    spatial_values,
    spatial_cotangent,
    temporal_queries,
    temporal_keys,
    temporal_values,
    temporal_cotangent,
    frame_bias,
    frame_count,
    grid_height,
    grid_width,
):
    hbm = pl.BlockSpec(memory_space=pl.ANY)
    smem = pl.BlockSpec(memory_space=pltpu.SMEM)
    vmem = pl.BlockSpec(memory_space=pltpu.VMEM)
    dma = pltpu.SemaphoreType.DMA
    spatial_shape = jax.ShapeDtypeStruct((PATCH, SP_HEADS * HEAD), BF16)
    temporal_shape = jax.ShapeDtypeStruct((PATCH + ROWS, TM_HEADS * HEAD), BF16)
    side = FRAMES * ROWS
    outs = pl.pallas_call(
        kernel,
        out_shape=(spatial_shape,) * 3
        + (temporal_shape,) * 3
        + (jax.ShapeDtypeStruct((TM_HEADS, 2 * FRAMES - 1), F32),),
        in_specs=[hbm] * 8 + [smem] * 4,
        out_specs=(hbm,) * 6 + (vmem,),
        scratch_shapes=[
            pltpu.VMEM((4, QPAD, SP_HEADS * HEAD), BF16),
            pltpu.VMEM((3, PATCH, SP_HEADS * HEAD), BF16),
            pltpu.VMEM((4, FRAMES, SLOTS * ROWS, HEAD), BF16),
            pltpu.VMEM((3, FRAMES, SLOTS * ROWS, HEAD), BF16),
            pltpu.VMEM((side, side), F32),
            pltpu.VMEM((side, side), F32),
            pltpu.VMEM((32, side), F32),
            pltpu.VMEM((DP, 32, HEAD), F32),
            pltpu.VMEM((FRAMES, 32, HEAD), F32),
            dma((GROUPS,)),
            dma((1,)),
            dma((1,)),
            dma((3,)),
            dma((3,)),
            dma((1,)),
            dma((1,)),
            dma((1,)),
            dma((1,)),
            dma((1,)),
            dma((1,)),
            dma((1,)),
        ],
        compiler_params=pltpu.CompilerParams(
            collective_id=0, has_side_effects=True, vmem_limit_bytes=56 << 20
        ),
        cost_estimate=pl.CostEstimate(
            flops=8_000_000_000, bytes_accessed=26_000_000, transcendentals=6_000_000
        ),
    )(
        spatial_queries[0, 0],
        spatial_keys[0, 0],
        spatial_values[0, 0],
        spatial_cotangent[0, 0],
        temporal_queries[0, 0],
        temporal_keys[0, 0],
        temporal_values[0, 0],
        temporal_cotangent[0, 0],
        frame_bias,
        frame_count,
        grid_height,
        grid_width,
    )
    spatial = tuple(o[None, None] for o in outs[:3])
    temporal = tuple(o[None, None, :PATCH] for o in outs[3:6])
    return spatial + temporal + (outs[6],)


def solution(mesh):
    split = P("dp", "seq", None, None)
    in_specs = (split,) * 8 + (P(),) + (P("dp"),) * 3
    out_specs = (split,) * 6 + (P(),)
    return jax.shard_map(
        per_device, mesh=mesh, in_specs=in_specs, out_specs=out_specs, check_vma=False
    )
```

```python
import functools
import math

import jax
import jax.numpy as jnp
from jax import lax
from jax.experimental import pallas as pl
from jax.experimental.pallas import tpu as pltpu
from jax.sharding import PartitionSpec as P

MESH = pl.DeviceIdType.MESH
HEAD = 128
GRID = 20
PATCH = 400
ROWS = 16
TILES = PATCH // ROWS
FRAMES = 16
SP_HEADS = 24
TM_HEADS = 12
SLOTS = 19
CHUNKS = ((0, 6), (6, 6), (12, 7))
GROUP = 3
GROUPS = SP_HEADS // GROUP
QPAD = 512
VMEM_LIMIT = 52 << 20
SCALE = 1.0 / math.sqrt(HEAD)
LOG2E = math.log2(math.e)
DEAD = -1e30
F32 = jnp.float32
BF16 = jnp.bfloat16

STEPS = (
    (2, 1, 0), (1, 0, 0), (3, 1, 0), (2, 0, 0), (1, 1, 0), (3, 0, 0), (0, 1, 0),
    (2, 0, 1), (2, 1, 1), (1, 0, 1), (3, 1, 1), (0, 0, 1), (1, 1, 1), (3, 0, 1), (0, 1, 1),
)


def dot(a, b, dims):
    return lax.dot_general(a, b, (dims, ((), ())), preferred_element_type=F32)


def attend(q, k, v, g, key_bias, query_live):
    scores = dot(k, q, ((1,), (1,))) * (SCALE * LOG2E) + key_bias
    weights = jnp.exp2(scores - jnp.max(scores, axis=0, keepdims=True))
    attention = weights * (query_live / jnp.sum(weights, axis=0, keepdims=True))
    low = attention.astype(BF16)
    grad_attention = dot(v, g, ((1,), (1,)))
    delta = jnp.sum(low.astype(F32) * grad_attention, axis=0, keepdims=True)
    grad_score = attention * (grad_attention - delta)
    grad_low = grad_score.astype(BF16)
    grad_value = dot(low, g, ((1,), (0,)))
    grad_key = dot(grad_low, q, ((1,), (0,))) * SCALE
    grad_query = dot(k, grad_low, ((0,), (0,))).T * SCALE
    return grad_query.astype(BF16), grad_key.astype(BF16), grad_value.astype(BF16), grad_score


def kernel(
    sq, sk, sv, sg, tq, tk, tv, tg, bias_in, count_in, height_in, width_in,
    osq, osk, osv, otq, otk, otv, table,
    held, recv, back, bias_mat, score_sum, bins, parts, by_x, sums, bias, count, height, width,
    small_sem, load_sem, out_sem, in_sem, own_sem, home_sem, home_recv, home_own,
    sum_send, sum_recv,
):
    me = lax.axis_index("seq")
    my_dp = lax.axis_index("dp")
    y, z, core = me // 4, (me // 2) % 2, me % 2
    spatial_in = (sq, sk, sv, sg)
    temporal_in, temporal_out = (tq, tk, tv, tg), (otq, otk, otv)

    def peer(step):
        return ((y + step[0]) % 4) * 4 + ((z + step[1]) % 2) * 2 + (core + step[2]) % 2

    def slot_of(step):
        return step[0] * 4 + step[1] * 2 + step[2]

    def unit_of(device, first):
        r = device % 4
        unit = SLOTS * r + first
        if first >= 12:
            unit = unit - r // 3
        return 3 * (device // 4) + unit // TILES, unit % TILES

    def tile_rows(tile, n):
        return pl.ds(pl.multiple_of(tile * ROWS, ROWS), n * ROWS)

    def head_cols(head):
        return pl.ds(pl.multiple_of(head * HEAD, HEAD), HEAD)

    barrier = pltpu.get_barrier_semaphore()
    for step in STEPS:
        pl.semaphore_signal(barrier, inc=1, device_id={"seq": peer(step)}, device_id_type=MESH)
    my_x, my_z = my_dp // 2, my_dp % 2
    pair = my_x * 2 + 1 - my_z
    across = [((my_x + i) % 4) * 2 + my_z for i in range(1, 4)]
    for other in [pair] + across:
        pl.semaphore_signal(barrier, inc=1, device_id={"dp": other}, device_id_type=MESH)

    small = [
        pltpu.make_async_copy(source, target, small_sem.at[i])
        for i, (source, target) in enumerate(
            ((bias_in, bias), (count_in, count), (height_in, height), (width_in, width))
        )
    ]
    for copy in small:
        copy.start()

    def load(group, a):
        cols = pl.ds(pl.multiple_of(group * GROUP * HEAD, HEAD), GROUP * HEAD)
        return pltpu.make_async_copy(
            spatial_in[a].at[:, cols], held.at[a, pl.ds(0, PATCH), cols], load_sem.at[group]
        )

    @pl.loop(0, GROUPS)
    def _(group):
        for a in range(4):
            load(group, a).start()

    for c, (first, n) in enumerate(CHUNKS):
        head, tile = unit_of(me, first)
        for a in range(4):
            pltpu.make_async_copy(
                temporal_in[a].at[tile_rows(tile, n), head_cols(head)],
                recv.at[a, 0, pl.ds(first * ROWS, n * ROWS)],
                own_sem.at[c],
            ).start()

    pl.semaphore_wait(barrier, len(STEPS) + 1 + len(across))

    for c, (first, n) in enumerate(CHUNKS):
        for a in range(4):
            for step in STEPS:
                to = peer(step)
                head, tile = unit_of(to, first)
                pltpu.make_async_remote_copy(
                    src_ref=temporal_in[a].at[tile_rows(tile, n), head_cols(head)],
                    dst_ref=recv.at[a, slot_of(step), pl.ds(first * ROWS, n * ROWS)],
                    send_sem=out_sem.at[0],
                    recv_sem=in_sem.at[c],
                    device_id={"seq": to},
                    device_id_type=MESH,
                ).start()

    for copy in small:
        copy.wait()

    def inside(patch):
        row = (patch * 3277) >> 16
        return ((row < height[0]) & (patch - row * GRID < width[0])).astype(F32)

    def frame_of(slot):
        dy, dz, dc = slot >> 2, (slot >> 1) & 1, slot & 1
        return ((y - dy) & 3) * 4 + ((z + dz) & 1) * 2 + ((core + dc) & 1)

    alive = (me < count[0]).astype(F32)
    key_live = inside(lax.broadcasted_iota(jnp.int32, (PATCH, 1), 0)) * alive
    key_bias = (1.0 - key_live) * DEAD
    queries = lax.broadcasted_iota(jnp.int32, (1, QPAD), 1)
    query_live = inside(queries) * alive * (queries < PATCH).astype(F32)

    held[0, pl.ds(PATCH, QPAD - PATCH), :] = jnp.zeros((QPAD - PATCH, SP_HEADS * HEAD), BF16)
    held[3, pl.ds(PATCH, QPAD - PATCH), :] = jnp.zeros((QPAD - PATCH, SP_HEADS * HEAD), BF16)
    bins[...] = jnp.zeros_like(bins)
    parts[0] = jnp.zeros(parts.shape[1:], F32)

    def spatial(start, stop):
        @pl.loop(start, stop)
        def _(group):
            cols = pl.ds(pl.multiple_of(group * GROUP * HEAD, HEAD), GROUP * HEAD)
            arrived = held.at[:, pl.ds(0, PATCH), cols]
            pltpu.make_async_copy(arrived, arrived, load_sem.at[group]).wait()

            @pl.loop(0, GROUP)
            def _(j):
                own = head_cols(group * GROUP + j)
                grads = attend(
                    held[0, :, own],
                    held[1, pl.ds(0, PATCH), own],
                    held[2, pl.ds(0, PATCH), own],
                    held[3, :, own],
                    key_bias,
                    query_live,
                )
                osq[:, own] = grads[0][:PATCH]
                osk[:, own] = grads[1]
                osv[:, own] = grads[2]

    def temporal(c):
        first, n = CHUNKS[c]
        head, tile = unit_of(me, first)
        side = FRAMES * ROWS
        key_at = lax.broadcasted_iota(jnp.int32, (side, 1), 0)
        query_at = lax.broadcasted_iota(jnp.int32, (1, side), 1)
        key_frame, query_frame = frame_of(key_at >> 4), frame_of(query_at >> 4)
        same = (key_at & 15) == (query_at & 15)
        apart = jnp.where(same, key_frame - query_frame + (FRAMES - 1), -1)
        frame_dead = jnp.where(key_frame < count[0], 0.0, DEAD)
        bias_mat[...] = jnp.where(same, frame_dead, DEAD)

        bias_row = bias[pl.ds(head, 1), :] * LOG2E
        bias_lane = lax.broadcasted_iota(jnp.int32, bias_row.shape, 1)

        @pl.loop(0, 2 * FRAMES - 1)
        def _(d):
            value = jnp.sum(jnp.where(bias_lane == d, bias_row, 0.0), axis=1, keepdims=True)
            bias_mat[...] += jnp.where(apart == d, value, 0.0)

        score_sum[...] = jnp.zeros_like(score_sum)

        own, arrived = recv.at[:, 0], recv.at[:, pl.ds(1, FRAMES - 1)]
        rows = pl.ds(first * ROWS, n * ROWS)
        own, arrived = own.at[:, rows], arrived.at[:, :, rows]
        pltpu.make_async_copy(own, own, own_sem.at[c]).wait()
        pltpu.make_async_copy(arrived, arrived, in_sem.at[c]).wait()

        @pl.loop(0, n)
        def _(i):
            slot_rows = pl.ds(pl.multiple_of((first + i) * ROWS, ROWS), ROWS)
            patch = (tile + i) * ROWS + (query_at & 15)
            live = inside(patch) * (query_frame < count[0]).astype(F32)
            if first >= 12:
                live = live * (1 - (me % 4) // 3 * (i < 1).astype(jnp.int32)).astype(F32)
            q, k, v, g = (
                recv[a, :, slot_rows, :].reshape(side, HEAD) for a in range(4)
            )
            grads = attend(q, k, v, g, bias_mat[...], live)
            score_sum[...] += grads[3]
            for a in range(3):
                back[a, :, slot_rows, :] = grads[a].reshape(FRAMES, ROWS, HEAD)

        folded = jnp.sum(score_sum[...].reshape(FRAMES, ROWS, side), axis=1)
        slots = lax.broadcasted_iota(jnp.int32, (FRAMES, 1), 0)
        distance = frame_of(slots) - query_frame + (FRAMES - 1)

        @pl.loop(0, 2 * FRAMES - 1)
        def _(d):
            bins[pl.ds(d, 1), :] = jnp.sum(
                jnp.where(distance == d, folded, 0.0), axis=0, keepdims=True
            )

        column = jnp.sum(bins[...], axis=1, keepdims=True)
        lanes = lax.broadcasted_iota(jnp.int32, (1, HEAD), 1)
        parts[0] += jnp.where(lanes == head, column, 0.0)

    def home(c, arrays=(0, 1, 2)):
        first, n = CHUNKS[c]
        head, tile = unit_of(me, first)
        pieces = [(first, 6, tile)]
        if n == 7:
            spare = (me % 4) // 3
            pieces = [(first + 1, 6, tile + 1), (first, 1, tile * (1 - spare) + TILES * spare)]
        for slot, size, at in pieces:
            rows = pl.ds(slot * ROWS, size * ROWS)
            for a in arrays:
                pltpu.make_async_copy(
                    back.at[a, 0, rows],
                    temporal_out[a].at[tile_rows(at, size), head_cols(head)],
                    home_own.at[0],
                ).start()
            for a in arrays:
                for step in STEPS:
                    from_slot = ((4 - step[0]) % 4) * 4 + step[1] * 2 + step[2]
                    pltpu.make_async_remote_copy(
                        src_ref=back.at[a, from_slot, rows],
                        dst_ref=temporal_out[a].at[tile_rows(at, size), head_cols(head)],
                        send_sem=home_sem.at[0],
                        recv_sem=home_recv.at[0],
                        device_id={"seq": peer(step)},
                        device_id_type=MESH,
                    ).start()

    spatial(0, 4)
    temporal(0)
    home(0)
    spatial(4, GROUPS)
    temporal(1)
    home(1)
    temporal(2)

    pair_copy = pltpu.make_async_remote_copy(
        src_ref=parts.at[0],
        dst_ref=parts.at[1],
        send_sem=sum_send.at[0],
        recv_sem=sum_recv.at[0],
        device_id={"dp": pair},
        device_id_type=MESH,
    )
    pair_copy.start()
    home(2, (0,))
    pair_copy.wait()
    by_x[my_x] = parts[0] + parts[1]
    for other in across:
        pltpu.make_async_remote_copy(
            src_ref=by_x.at[my_x],
            dst_ref=by_x.at[my_x],
            send_sem=sum_send.at[1],
            recv_sem=sum_recv.at[1],
            device_id={"dp": other},
            device_id_type=MESH,
        ).start()
    home(2, (1,))
    three = by_x.at[pl.ds(0, 3)]
    pltpu.make_async_copy(three, three, sum_recv.at[1]).wait()
    pltpu.make_async_copy(three, three, sum_send.at[1]).wait()
    sums[0] = (by_x[0] + by_x[1]) + (by_x[2] + by_x[3])
    for step in STEPS:
        pltpu.make_async_remote_copy(
            src_ref=sums.at[0],
            dst_ref=sums.at[slot_of(step)],
            send_sem=sum_send.at[2],
            recv_sem=sum_recv.at[2],
            device_id={"seq": peer(step)},
            device_id_type=MESH,
        ).start()
    home(2, (2,))
    others = sums.at[pl.ds(1, FRAMES - 1)]
    pltpu.make_async_copy(others, others, sum_recv.at[2]).wait()
    pltpu.make_async_copy(others, others, sum_send.at[2]).wait()
    total = functools.reduce(jnp.add, [sums[i] for i in range(FRAMES)])
    wide = jnp.concatenate([total, jnp.zeros((HEAD - total.shape[0], HEAD), F32)], axis=0)
    table[...] = wide.T[:ROWS]

    sent = recv.at[:, pl.ds(1, FRAMES - 1)]
    pltpu.make_async_copy(sent, sent, out_sem.at[0]).wait()
    own, others = back.at[:, 0], back.at[:, pl.ds(1, FRAMES - 1)]
    pltpu.make_async_copy(own, own, home_own.at[0]).wait()
    pltpu.make_async_copy(others, others, home_sem.at[0]).wait()
    pltpu.make_async_copy(others, others, home_recv.at[0]).wait()


def store_kernel(*refs):
    copies = [
        pltpu.make_async_copy(made.at[pl.ds(0, PATCH)], out, refs[14].at[i])
        for i, (made, out) in enumerate(zip(refs[:6], refs[7:13]))
    ]
    for copy in copies:
        copy.start()
    refs[13][...] = refs[6][:TM_HEADS, : 2 * FRAMES - 1]
    for copy in copies:
        copy.wait()


def per_device(
    spatial_queries,
    spatial_keys,
    spatial_values,
    spatial_cotangent,
    temporal_queries,
    temporal_keys,
    temporal_values,
    temporal_cotangent,
    frame_bias,
    frame_count,
    grid_height,
    grid_width,
):
    hbm = pl.BlockSpec(memory_space=pl.ANY)
    vmem = pl.BlockSpec(memory_space=pltpu.VMEM)
    dma = pltpu.SemaphoreType.DMA
    spatial_shape = pltpu.VMEM((PATCH, SP_HEADS * HEAD), BF16)
    temporal_shape = pltpu.VMEM((PATCH + ROWS, TM_HEADS * HEAD), BF16)
    side = FRAMES * ROWS
    outs = pl.pallas_call(
        kernel,
        out_shape=(spatial_shape,) * 3
        + (temporal_shape,) * 3
        + (pltpu.VMEM((ROWS, HEAD), F32),),
        in_specs=[hbm] * 12,
        out_specs=(vmem,) * 7,
        scratch_shapes=[
            pltpu.VMEM((4, QPAD, SP_HEADS * HEAD), BF16),
            pltpu.VMEM((4, FRAMES, SLOTS * ROWS, HEAD), BF16),
            pltpu.VMEM((3, FRAMES, SLOTS * ROWS, HEAD), BF16),
            pltpu.VMEM((side, side), F32),
            pltpu.VMEM((side, side), F32),
            pltpu.VMEM((32, side), F32),
            pltpu.VMEM((2, 32, HEAD), F32),
            pltpu.VMEM((4, 32, HEAD), F32),
            pltpu.VMEM((FRAMES, 32, HEAD), F32),
            pltpu.VMEM((TM_HEADS, 2 * FRAMES - 1), F32),
            pltpu.SMEM((1,), jnp.int32),
            pltpu.SMEM((1,), jnp.int32),
            pltpu.SMEM((1,), jnp.int32),
            dma((4,)),
            dma((GROUPS,)),
            dma((1,)),
            dma((3,)),
            dma((3,)),
            dma((1,)),
            dma((1,)),
            dma((1,)),
            dma((3,)),
            dma((3,)),
        ],
        compiler_params=pltpu.CompilerParams(
            collective_id=0, has_side_effects=True, vmem_limit_bytes=VMEM_LIMIT
        ),
        cost_estimate=pl.CostEstimate(
            flops=8_000_000_000, bytes_accessed=26_000_000, transcendentals=6_000_000
        ),
    )(
        spatial_queries[0, 0],
        spatial_keys[0, 0],
        spatial_values[0, 0],
        spatial_cotangent[0, 0],
        temporal_queries[0, 0],
        temporal_keys[0, 0],
        temporal_values[0, 0],
        temporal_cotangent[0, 0],
        frame_bias,
        frame_count,
        grid_height,
        grid_width,
    )
    stored = pl.pallas_call(
        store_kernel,
        out_shape=tuple(
            jax.ShapeDtypeStruct((PATCH, heads * HEAD), BF16)
            for heads in (SP_HEADS,) * 3 + (TM_HEADS,) * 3
        )
        + (jax.ShapeDtypeStruct((TM_HEADS, 2 * FRAMES - 1), F32),),
        in_specs=[vmem] * 7,
        out_specs=(hbm,) * 6 + (vmem,),
        scratch_shapes=[dma((6,))],
        compiler_params=pltpu.CompilerParams(vmem_limit_bytes=1 << 20),
        cost_estimate=pl.CostEstimate(flops=0, bytes_accessed=11_000_000, transcendentals=0),
    )(*outs)
    return tuple(o[None, None] for o in stored[:6]) + (stored[6],)


def solution(mesh):
    split = P("dp", "seq", None, None)
    in_specs = (split,) * 8 + (P(),) + (P("dp"),) * 3
    out_specs = (split,) * 6 + (P(),)
    return jax.shard_map(
        per_device, mesh=mesh, in_specs=in_specs, out_specs=out_specs, check_vma=False
    )
```

```python
import functools
import math

import jax
import jax.numpy as jnp
from jax import lax
from jax.experimental import pallas as pl
from jax.experimental.pallas import tpu as pltpu
from jax.sharding import PartitionSpec as P

MESH = pl.DeviceIdType.MESH
HEAD = 128
GRID = 20
PATCH = 400
ROWS = 16
TILES = PATCH // ROWS
FRAMES = 16
SP_HEADS = 24
TM_HEADS = 12
SLOTS = 19
CHUNKS = ((0, 6), (6, 6), (12, 7))
GROUP = 3
GROUPS = SP_HEADS // GROUP
QPAD = 512
VMEM_LIMIT = 52 << 20
SCALE = 1.0 / math.sqrt(HEAD)
LOG2E = math.log2(math.e)
DEAD = -1e30
F32 = jnp.float32
BF16 = jnp.bfloat16

STEPS = (
    (2, 1, 0), (1, 0, 0), (3, 1, 0), (2, 0, 0), (1, 1, 0), (3, 0, 0), (0, 1, 0),
    (2, 0, 1), (2, 1, 1), (1, 0, 1), (3, 1, 1), (0, 0, 1), (1, 1, 1), (3, 0, 1), (0, 1, 1),
)


def dot(a, b, dims):
    return lax.dot_general(a, b, (dims, ((), ())), preferred_element_type=F32)


def attend(q, k, v, g, key_bias, query_live):
    scores = dot(k, q, ((1,), (1,))) * (SCALE * LOG2E) + key_bias
    weights = jnp.exp2(scores - jnp.max(scores, axis=0, keepdims=True))
    attention = weights * (query_live / jnp.sum(weights, axis=0, keepdims=True))
    low = attention.astype(BF16)
    grad_attention = dot(v, g, ((1,), (1,)))
    delta = jnp.sum(low.astype(F32) * grad_attention, axis=0, keepdims=True)
    grad_score = attention * (grad_attention - delta)
    grad_low = grad_score.astype(BF16)
    grad_value = dot(low, g, ((1,), (0,)))
    grad_key = dot(grad_low, q, ((1,), (0,))) * SCALE
    grad_query = dot(k, grad_low, ((0,), (0,))).T * SCALE
    return grad_query.astype(BF16), grad_key.astype(BF16), grad_value.astype(BF16), grad_score


def kernel(
    sq, sk, sv, sg, tq, tk, tv, tg, bias_in, count_in, height_in, width_in,
    osq, osk, osv, otq, otk, otv, table,
    held, recv, back, bias_mat, score_sum, bins, parts, by_x, sums, bias, count, height, width,
    small_sem, load_sem, out_sem, in_sem, own_sem, home_sem, home_recv, home_own,
    sum_send, sum_recv,
):
    me = lax.axis_index("seq")
    my_dp = lax.axis_index("dp")
    y, z, core = me // 4, (me // 2) % 2, me % 2
    spatial_in = (sq, sk, sv, sg)
    temporal_in, temporal_out = (tq, tk, tv, tg), (otq, otk, otv)

    def peer(step):
        return ((y + step[0]) % 4) * 4 + ((z + step[1]) % 2) * 2 + (core + step[2]) % 2

    def slot_of(step):
        return step[0] * 4 + step[1] * 2 + step[2]

    def unit_of(device, first):
        r = device % 4
        unit = SLOTS * r + first
        if first >= 12:
            unit = unit - r // 3
        return 3 * (device // 4) + unit // TILES, unit % TILES

    def tile_rows(tile, n):
        return pl.ds(pl.multiple_of(tile * ROWS, ROWS), n * ROWS)

    def head_cols(head):
        return pl.ds(pl.multiple_of(head * HEAD, HEAD), HEAD)

    barrier = pltpu.get_barrier_semaphore()
    for step in STEPS:
        pl.semaphore_signal(barrier, inc=1, device_id={"seq": peer(step)}, device_id_type=MESH)
    my_x, my_z = my_dp // 2, my_dp % 2
    pair = my_x * 2 + 1 - my_z
    across = [((my_x + i) % 4) * 2 + my_z for i in range(1, 4)]
    for other in [pair] + across:
        pl.semaphore_signal(barrier, inc=1, device_id={"dp": other}, device_id_type=MESH)

    small = [
        pltpu.make_async_copy(source, target, small_sem.at[i])
        for i, (source, target) in enumerate(
            ((bias_in, bias), (count_in, count), (height_in, height), (width_in, width))
        )
    ]
    for copy in small:
        copy.start()

    def load(group, a):
        cols = pl.ds(pl.multiple_of(group * GROUP * HEAD, HEAD), GROUP * HEAD)
        return pltpu.make_async_copy(
            spatial_in[a].at[:, cols], held.at[a, pl.ds(0, PATCH), cols], load_sem.at[group]
        )

    @pl.loop(0, GROUPS)
    def _(group):
        for a in range(4):
            load(group, a).start()

    for c, (first, n) in enumerate(CHUNKS):
        head, tile = unit_of(me, first)
        for a in range(4):
            pltpu.make_async_copy(
                temporal_in[a].at[tile_rows(tile, n), head_cols(head)],
                recv.at[a, 0, pl.ds(first * ROWS, n * ROWS)],
                own_sem.at[c],
            ).start()

    pl.semaphore_wait(barrier, len(STEPS) + 1 + len(across))

    for c, (first, n) in enumerate(CHUNKS):
        for a in range(4):
            for step in STEPS:
                to = peer(step)
                head, tile = unit_of(to, first)
                pltpu.make_async_remote_copy(
                    src_ref=temporal_in[a].at[tile_rows(tile, n), head_cols(head)],
                    dst_ref=recv.at[a, slot_of(step), pl.ds(first * ROWS, n * ROWS)],
                    send_sem=out_sem.at[0],
                    recv_sem=in_sem.at[c],
                    device_id={"seq": to},
                    device_id_type=MESH,
                ).start()

    for copy in small:
        copy.wait()

    def inside(patch):
        row = (patch * 3277) >> 16
        return ((row < height[0]) & (patch - row * GRID < width[0])).astype(F32)

    def frame_of(slot):
        dy, dz, dc = slot >> 2, (slot >> 1) & 1, slot & 1
        return ((y - dy) & 3) * 4 + ((z + dz) & 1) * 2 + ((core + dc) & 1)

    alive = (me < count[0]).astype(F32)
    key_live = inside(lax.broadcasted_iota(jnp.int32, (PATCH, 1), 0)) * alive
    key_bias = (1.0 - key_live) * DEAD
    queries = lax.broadcasted_iota(jnp.int32, (1, QPAD), 1)
    query_live = inside(queries) * alive * (queries < PATCH).astype(F32)

    held[0, pl.ds(PATCH, QPAD - PATCH), :] = jnp.zeros((QPAD - PATCH, SP_HEADS * HEAD), BF16)
    held[3, pl.ds(PATCH, QPAD - PATCH), :] = jnp.zeros((QPAD - PATCH, SP_HEADS * HEAD), BF16)
    bins[...] = jnp.zeros_like(bins)
    parts[0] = jnp.zeros(parts.shape[1:], F32)

    def spatial(start, stop):
        @pl.loop(start, stop)
        def _(group):
            cols = pl.ds(pl.multiple_of(group * GROUP * HEAD, HEAD), GROUP * HEAD)
            arrived = held.at[:, pl.ds(0, PATCH), cols]
            pltpu.make_async_copy(arrived, arrived, load_sem.at[group]).wait()

            @pl.loop(0, GROUP)
            def _(j):
                own = head_cols(group * GROUP + j)
                grads = attend(
                    held[0, :, own],
                    held[1, pl.ds(0, PATCH), own],
                    held[2, pl.ds(0, PATCH), own],
                    held[3, :, own],
                    key_bias,
                    query_live,
                )
                osq[:, own] = grads[0][:PATCH]
                osk[:, own] = grads[1]
                osv[:, own] = grads[2]

    def temporal(c):
        first, n = CHUNKS[c]
        head, tile = unit_of(me, first)
        side = FRAMES * ROWS
        key_at = lax.broadcasted_iota(jnp.int32, (side, 1), 0)
        query_at = lax.broadcasted_iota(jnp.int32, (1, side), 1)
        key_frame, query_frame = frame_of(key_at >> 4), frame_of(query_at >> 4)
        same = (key_at & 15) == (query_at & 15)
        apart = jnp.where(same, key_frame - query_frame + (FRAMES - 1), -1)
        frame_dead = jnp.where(key_frame < count[0], 0.0, DEAD)
        bias_mat[...] = jnp.where(same, frame_dead, DEAD)

        bias_row = bias[pl.ds(head, 1), :] * LOG2E
        bias_lane = lax.broadcasted_iota(jnp.int32, bias_row.shape, 1)

        @pl.loop(0, 2 * FRAMES - 1)
        def _(d):
            value = jnp.sum(jnp.where(bias_lane == d, bias_row, 0.0), axis=1, keepdims=True)
            bias_mat[...] += jnp.where(apart == d, value, 0.0)

        score_sum[...] = jnp.zeros_like(score_sum)

        own, arrived = recv.at[:, 0], recv.at[:, pl.ds(1, FRAMES - 1)]
        rows = pl.ds(first * ROWS, n * ROWS)
        own, arrived = own.at[:, rows], arrived.at[:, :, rows]
        pltpu.make_async_copy(own, own, own_sem.at[c]).wait()
        pltpu.make_async_copy(arrived, arrived, in_sem.at[c]).wait()

        @pl.loop(0, n)
        def _(i):
            slot_rows = pl.ds(pl.multiple_of((first + i) * ROWS, ROWS), ROWS)
            patch = (tile + i) * ROWS + (query_at & 15)
            live = inside(patch) * (query_frame < count[0]).astype(F32)
            if first >= 12:
                live = live * (1 - (me % 4) // 3 * (i < 1).astype(jnp.int32)).astype(F32)
            q, k, v, g = (
                recv[a, :, slot_rows, :].reshape(side, HEAD) for a in range(4)
            )
            grads = attend(q, k, v, g, bias_mat[...], live)
            score_sum[...] += grads[3]
            for a in range(3):
                back[a, :, slot_rows, :] = grads[a].reshape(FRAMES, ROWS, HEAD)

        folded = jnp.sum(score_sum[...].reshape(FRAMES, ROWS, side), axis=1)
        slots = lax.broadcasted_iota(jnp.int32, (FRAMES, 1), 0)
        distance = frame_of(slots) - query_frame + (FRAMES - 1)

        @pl.loop(0, 2 * FRAMES - 1)
        def _(d):
            bins[pl.ds(d, 1), :] = jnp.sum(
                jnp.where(distance == d, folded, 0.0), axis=0, keepdims=True
            )

        halves = bins[:, :HEAD] + bins[:, HEAD:]
        wide = jnp.concatenate([halves, jnp.zeros((HEAD - 32, HEAD), F32)], axis=0)
        line = jnp.sum(wide.T, axis=0, keepdims=True)
        rows_at = lax.broadcasted_iota(jnp.int32, (8, 1), 0)
        parts[0] += jnp.where(rows_at == head - 3 * y, line, 0.0)

    def home(c, arrays=(0, 1, 2)):
        first, n = CHUNKS[c]
        head, tile = unit_of(me, first)
        pieces = [(first, 6, tile)]
        if n == 7:
            spare = (me % 4) // 3
            pieces = [(first + 1, 6, tile + 1), (first, 1, tile * (1 - spare) + TILES * spare)]
        for slot, size, at in pieces:
            rows = pl.ds(slot * ROWS, size * ROWS)
            for a in arrays:
                pltpu.make_async_copy(
                    back.at[a, 0, rows],
                    temporal_out[a].at[tile_rows(at, size), head_cols(head)],
                    home_own.at[0],
                ).start()
            for a in arrays:
                for step in STEPS:
                    from_slot = ((4 - step[0]) % 4) * 4 + step[1] * 2 + step[2]
                    pltpu.make_async_remote_copy(
                        src_ref=back.at[a, from_slot, rows],
                        dst_ref=temporal_out[a].at[tile_rows(at, size), head_cols(head)],
                        send_sem=home_sem.at[0],
                        recv_sem=home_recv.at[0],
                        device_id={"seq": peer(step)},
                        device_id_type=MESH,
                    ).start()

    spatial(0, 4)
    temporal(0)
    home(0)
    spatial(4, GROUPS)
    temporal(1)
    home(1, (0,))
    temporal(2)

    pair_copy = pltpu.make_async_remote_copy(
        src_ref=parts.at[0],
        dst_ref=parts.at[1],
        send_sem=sum_send.at[0],
        recv_sem=sum_recv.at[0],
        device_id={"dp": pair},
        device_id_type=MESH,
    )
    pair_copy.start()
    home(1, (1,))
    pair_copy.wait()
    by_x[my_x] = parts[0] + parts[1]
    for other in across:
        pltpu.make_async_remote_copy(
            src_ref=by_x.at[my_x],
            dst_ref=by_x.at[my_x],
            send_sem=sum_send.at[1],
            recv_sem=sum_recv.at[1],
            device_id={"dp": other},
            device_id_type=MESH,
        ).start()
    home(1, (2,))
    three = by_x.at[pl.ds(0, 3)]
    pltpu.make_async_copy(three, three, sum_recv.at[1]).wait()
    pltpu.make_async_copy(three, three, sum_send.at[1]).wait()
    sums[0] = (by_x[0] + by_x[1]) + (by_x[2] + by_x[3])
    for step in STEPS:
        pltpu.make_async_remote_copy(
            src_ref=sums.at[0],
            dst_ref=sums.at[slot_of(step)],
            send_sem=sum_send.at[2],
            recv_sem=sum_recv.at[2],
            device_id={"seq": peer(step)},
            device_id_type=MESH,
        ).start()
    home(2)
    others = sums.at[pl.ds(1, FRAMES - 1)]
    pltpu.make_async_copy(others, others, sum_recv.at[2]).wait()
    pltpu.make_async_copy(others, others, sum_send.at[2]).wait()
    for dy in range(4):
        table[(y + 4 - dy) % 4] = (sums[4 * dy] + sums[4 * dy + 1]) + (
            sums[4 * dy + 2] + sums[4 * dy + 3]
        )

    sent = recv.at[:, pl.ds(1, FRAMES - 1)]
    pltpu.make_async_copy(sent, sent, out_sem.at[0]).wait()
    own, others = back.at[:, 0], back.at[:, pl.ds(1, FRAMES - 1)]
    pltpu.make_async_copy(own, own, home_own.at[0]).wait()
    pltpu.make_async_copy(others, others, home_sem.at[0]).wait()
    pltpu.make_async_copy(others, others, home_recv.at[0]).wait()


def store_kernel(*refs):
    copies = [
        pltpu.make_async_copy(made.at[pl.ds(0, PATCH)], out, refs[14].at[i])
        for i, (made, out) in enumerate(zip(refs[:6], refs[7:13]))
    ]
    for copy in copies:
        copy.start()
    for row in range(4):
        refs[13][pl.ds(3 * row, 3), :] = refs[6][row, :3, : 2 * FRAMES - 1]
    for copy in copies:
        copy.wait()


def per_device(
    spatial_queries,
    spatial_keys,
    spatial_values,
    spatial_cotangent,
    temporal_queries,
    temporal_keys,
    temporal_values,
    temporal_cotangent,
    frame_bias,
    frame_count,
    grid_height,
    grid_width,
):
    hbm = pl.BlockSpec(memory_space=pl.ANY)
    vmem = pl.BlockSpec(memory_space=pltpu.VMEM)
    dma = pltpu.SemaphoreType.DMA
    spatial_shape = pltpu.VMEM((PATCH, SP_HEADS * HEAD), BF16)
    temporal_shape = pltpu.VMEM((PATCH + ROWS, TM_HEADS * HEAD), BF16)
    side = FRAMES * ROWS
    outs = pl.pallas_call(
        kernel,
        out_shape=(spatial_shape,) * 3
        + (temporal_shape,) * 3
        + (pltpu.VMEM((4, 8, HEAD), F32),),
        in_specs=[hbm] * 12,
        out_specs=(vmem,) * 7,
        scratch_shapes=[
            pltpu.VMEM((4, QPAD, SP_HEADS * HEAD), BF16),
            pltpu.VMEM((4, FRAMES, SLOTS * ROWS, HEAD), BF16),
            pltpu.VMEM((3, FRAMES, SLOTS * ROWS, HEAD), BF16),
            pltpu.VMEM((side, side), F32),
            pltpu.VMEM((side, side), F32),
            pltpu.VMEM((32, side), F32),
            pltpu.VMEM((2, 8, HEAD), F32),
            pltpu.VMEM((4, 8, HEAD), F32),
            pltpu.VMEM((FRAMES, 8, HEAD), F32),
            pltpu.VMEM((TM_HEADS, 2 * FRAMES - 1), F32),
            pltpu.SMEM((1,), jnp.int32),
            pltpu.SMEM((1,), jnp.int32),
            pltpu.SMEM((1,), jnp.int32),
            dma((4,)),
            dma((GROUPS,)),
            dma((1,)),
            dma((3,)),
            dma((3,)),
            dma((1,)),
            dma((1,)),
            dma((1,)),
            dma((3,)),
            dma((3,)),
        ],
        compiler_params=pltpu.CompilerParams(
            collective_id=0, has_side_effects=True, vmem_limit_bytes=VMEM_LIMIT
        ),
        cost_estimate=pl.CostEstimate(
            flops=8_000_000_000, bytes_accessed=26_000_000, transcendentals=6_000_000
        ),
    )(
        spatial_queries[0, 0],
        spatial_keys[0, 0],
        spatial_values[0, 0],
        spatial_cotangent[0, 0],
        temporal_queries[0, 0],
        temporal_keys[0, 0],
        temporal_values[0, 0],
        temporal_cotangent[0, 0],
        frame_bias,
        frame_count,
        grid_height,
        grid_width,
    )
    stored = pl.pallas_call(
        store_kernel,
        out_shape=tuple(
            jax.ShapeDtypeStruct((PATCH, heads * HEAD), BF16)
            for heads in (SP_HEADS,) * 3 + (TM_HEADS,) * 3
        )
        + (jax.ShapeDtypeStruct((TM_HEADS, 2 * FRAMES - 1), F32),),
        in_specs=[vmem] * 7,
        out_specs=(hbm,) * 6 + (vmem,),
        scratch_shapes=[dma((6,))],
        compiler_params=pltpu.CompilerParams(vmem_limit_bytes=1 << 20),
        cost_estimate=pl.CostEstimate(flops=0, bytes_accessed=11_000_000, transcendentals=0),
    )(*outs)
    return tuple(o[None, None] for o in stored[:6]) + (stored[6],)


def solution(mesh):
    split = P("dp", "seq", None, None)
    in_specs = (split,) * 8 + (P(),) + (P("dp"),) * 3
    out_specs = (split,) * 6 + (P(),)
    return jax.shard_map(
        per_device, mesh=mesh, in_specs=in_specs, out_specs=out_specs, check_vma=False
    )
```

```python
import functools
import math

import jax
import jax.numpy as jnp
from jax import lax
from jax.experimental import pallas as pl
from jax.experimental.pallas import tpu as pltpu
from jax.sharding import PartitionSpec as P

MESH = pl.DeviceIdType.MESH
HEAD = 128
GRID = 20
PATCH = 400
ROWS = 16
TILES = PATCH // ROWS
FRAMES = 16
SP_HEADS = 24
TM_HEADS = 12
SLOTS = 19
CHUNKS = ((0, 6), (6, 6), (12, 7))
GROUP = 3
GROUPS = SP_HEADS // GROUP
QPAD = 512
VMEM_LIMIT = 52 << 20
SCALE = 1.0 / math.sqrt(HEAD)
LOG2E = math.log2(math.e)
DEAD = -1e30
F32 = jnp.float32
BF16 = jnp.bfloat16

STEPS = (
    (2, 1, 0), (1, 0, 0), (3, 1, 0), (2, 0, 0), (1, 1, 0), (3, 0, 0), (0, 1, 0),
    (2, 0, 1), (2, 1, 1), (1, 0, 1), (3, 1, 1), (0, 0, 1), (1, 1, 1), (3, 0, 1), (0, 1, 1),
)


def dot(a, b, dims):
    return lax.dot_general(a, b, (dims, ((), ())), preferred_element_type=F32)


def attend(q, k, v, g, key_bias, query_live):
    scores = dot(k, q, ((1,), (1,))) * (SCALE * LOG2E) + key_bias
    weights = jnp.exp2(scores - jnp.max(scores, axis=0, keepdims=True))
    attention = weights * (query_live / jnp.sum(weights, axis=0, keepdims=True))
    low = attention.astype(BF16)
    grad_attention = dot(v, g, ((1,), (1,)))
    delta = jnp.sum(low.astype(F32) * grad_attention, axis=0, keepdims=True)
    grad_score = attention * (grad_attention - delta)
    grad_low = grad_score.astype(BF16)
    grad_value = dot(low, g, ((1,), (0,)))
    grad_key = dot(grad_low, q, ((1,), (0,))) * SCALE
    grad_query = dot(k, grad_low, ((0,), (0,))).T * SCALE
    return grad_query.astype(BF16), grad_key.astype(BF16), grad_value.astype(BF16), grad_score


def kernel(
    sq, sk, sv, sg, tq, tk, tv, tg, bias_in, count_in, height_in, width_in,
    osq, osk, osv, otq, otk, otv, table,
    held, recv, back, bias_mat, score_sum, bins, parts, by_x, sums, bias, count, height, width,
    small_sem, load_sem, out_sem, in_sem, own_sem, home_sem, home_recv, home_own,
    sum_send, sum_recv,
):
    me = lax.axis_index("seq")
    my_dp = lax.axis_index("dp")
    y, z, core = me // 4, (me // 2) % 2, me % 2
    spatial_in = (sq, sk, sv, sg)
    temporal_in, temporal_out = (tq, tk, tv, tg), (otq, otk, otv)

    def along_y(step):
        return (step[0] + core * (4 - 2 * step[0])) % 4

    def peer(step):
        return ((y + along_y(step)) % 4) * 4 + ((z + step[1]) % 2) * 2 + (core + step[2]) % 2

    def slot_of(step):
        return along_y(step) * 4 + step[1] * 2 + step[2]

    def role_of(device):
        r = device % 4
        return r + (device // 4) % 2 * (3 - 2 * r)

    role = role_of(me)

    def unit_of(device, first):
        role = role_of(device)
        unit = SLOTS * role + first
        if first >= 12:
            unit = unit - role // 3
        return 3 * (device // 4) + unit // TILES, unit % TILES

    def tile_rows(tile, n):
        return pl.ds(pl.multiple_of(tile * ROWS, ROWS), n * ROWS)

    def head_cols(head):
        return pl.ds(pl.multiple_of(head * HEAD, HEAD), HEAD)

    barrier = pltpu.get_barrier_semaphore()
    for step in STEPS:
        pl.semaphore_signal(barrier, inc=1, device_id={"seq": peer(step)}, device_id_type=MESH)
    my_x, my_z = my_dp // 2, my_dp % 2
    pair = my_x * 2 + 1 - my_z
    across = [((my_x + i) % 4) * 2 + my_z for i in range(1, 4)]
    for other in [pair] + across:
        pl.semaphore_signal(barrier, inc=1, device_id={"dp": other}, device_id_type=MESH)

    small = [
        pltpu.make_async_copy(source, target, small_sem.at[i])
        for i, (source, target) in enumerate(
            ((bias_in, bias), (count_in, count), (height_in, height), (width_in, width))
        )
    ]
    for copy in small:
        copy.start()

    def load(group, a):
        cols = pl.ds(pl.multiple_of(group * GROUP * HEAD, HEAD), GROUP * HEAD)
        return pltpu.make_async_copy(
            spatial_in[a].at[:, cols], held.at[a, pl.ds(0, PATCH), cols], load_sem.at[group]
        )

    @pl.loop(0, GROUPS)
    def _(group):
        for a in range(4):
            load(group, a).start()

    for c, (first, n) in enumerate(CHUNKS):
        head, tile = unit_of(me, first)
        for a in range(4):
            pltpu.make_async_copy(
                temporal_in[a].at[tile_rows(tile, n), head_cols(head)],
                recv.at[a, 0, pl.ds(first * ROWS, n * ROWS)],
                own_sem.at[c],
            ).start()

    pl.semaphore_wait(barrier, len(STEPS) + 1 + len(across))

    for c, (first, n) in enumerate(CHUNKS):
        for a in range(4):
            for step in STEPS:
                to = peer(step)
                head, tile = unit_of(to, first)
                extra = n - 6
                pltpu.make_async_remote_copy(
                    src_ref=temporal_in[a].at[tile_rows(tile + extra, 6), head_cols(head)],
                    dst_ref=recv.at[a, slot_of(step), pl.ds((first + extra) * ROWS, 6 * ROWS)],
                    send_sem=out_sem.at[0],
                    recv_sem=in_sem.at[c],
                    device_id={"seq": to},
                    device_id_type=MESH,
                ).start()
                if extra:

                    @pl.when(role_of(to) != 3)
                    def _():
                        pltpu.make_async_remote_copy(
                            src_ref=temporal_in[a].at[tile_rows(tile, 1), head_cols(head)],
                            dst_ref=recv.at[a, slot_of(step), pl.ds(first * ROWS, ROWS)],
                            send_sem=out_sem.at[1],
                            recv_sem=in_sem.at[3],
                            device_id={"seq": to},
                            device_id_type=MESH,
                        ).start()

    for copy in small:
        copy.wait()

    def inside(patch):
        row = (patch * 3277) >> 16
        return ((row < height[0]) & (patch - row * GRID < width[0])).astype(F32)

    def frame_of(slot):
        dy, dz, dc = slot >> 2, (slot >> 1) & 1, slot & 1
        return ((y - dy) & 3) * 4 + ((z + dz) & 1) * 2 + ((core + dc) & 1)

    alive = (me < count[0]).astype(F32)
    key_live = inside(lax.broadcasted_iota(jnp.int32, (PATCH, 1), 0)) * alive
    key_bias = (1.0 - key_live) * DEAD
    queries = lax.broadcasted_iota(jnp.int32, (1, QPAD), 1)
    query_live = inside(queries) * alive * (queries < PATCH).astype(F32)

    held[0, pl.ds(PATCH, QPAD - PATCH), :] = jnp.zeros((QPAD - PATCH, SP_HEADS * HEAD), BF16)
    held[3, pl.ds(PATCH, QPAD - PATCH), :] = jnp.zeros((QPAD - PATCH, SP_HEADS * HEAD), BF16)
    bins[...] = jnp.zeros_like(bins)
    parts[0] = jnp.zeros(parts.shape[1:], F32)

    def spatial(start, stop):
        @pl.loop(start, stop)
        def _(group):
            cols = pl.ds(pl.multiple_of(group * GROUP * HEAD, HEAD), GROUP * HEAD)
            arrived = held.at[:, pl.ds(0, PATCH), cols]
            pltpu.make_async_copy(arrived, arrived, load_sem.at[group]).wait()

            @pl.loop(0, GROUP)
            def _(j):
                own = head_cols(group * GROUP + j)
                grads = attend(
                    held[0, :, own],
                    held[1, pl.ds(0, PATCH), own],
                    held[2, pl.ds(0, PATCH), own],
                    held[3, :, own],
                    key_bias,
                    query_live,
                )
                osq[:, own] = grads[0][:PATCH]
                osk[:, own] = grads[1]
                osv[:, own] = grads[2]

    def temporal(c):
        first, n = CHUNKS[c]
        head, tile = unit_of(me, first)
        side = FRAMES * ROWS
        key_at = lax.broadcasted_iota(jnp.int32, (side, 1), 0)
        query_at = lax.broadcasted_iota(jnp.int32, (1, side), 1)
        key_frame, query_frame = frame_of(key_at >> 4), frame_of(query_at >> 4)
        same = (key_at & 15) == (query_at & 15)
        apart = jnp.where(same, key_frame - query_frame + (FRAMES - 1), -1)
        frame_dead = jnp.where(key_frame < count[0], 0.0, DEAD)
        bias_mat[...] = jnp.where(same, frame_dead, DEAD)

        bias_row = bias[pl.ds(head, 1), :] * LOG2E
        bias_lane = lax.broadcasted_iota(jnp.int32, bias_row.shape, 1)

        @pl.loop(0, 2 * FRAMES - 1)
        def _(d):
            value = jnp.sum(jnp.where(bias_lane == d, bias_row, 0.0), axis=1, keepdims=True)
            bias_mat[...] += jnp.where(apart == d, value, 0.0)

        score_sum[...] = jnp.zeros_like(score_sum)

        extra = n - 6
        own = recv.at[:, 0, pl.ds(first * ROWS, n * ROWS)]
        arrived = recv.at[:, pl.ds(1, FRAMES - 1), pl.ds((first + extra) * ROWS, 6 * ROWS)]
        pltpu.make_async_copy(own, own, own_sem.at[c]).wait()
        pltpu.make_async_copy(arrived, arrived, in_sem.at[c]).wait()
        if extra:

            @pl.when(role != 3)
            def _():
                tile_arrived = recv.at[:, pl.ds(1, FRAMES - 1), pl.ds(first * ROWS, ROWS)]
                pltpu.make_async_copy(tile_arrived, tile_arrived, in_sem.at[3]).wait()

        @pl.loop(role // 3 if extra else 0, n)
        def _(i):
            slot_rows = pl.ds(pl.multiple_of((first + i) * ROWS, ROWS), ROWS)
            patch = (tile + i) * ROWS + (query_at & 15)
            live = inside(patch) * (query_frame < count[0]).astype(F32)
            q, k, v, g = (
                recv[a, :, slot_rows, :].reshape(side, HEAD) for a in range(4)
            )
            grads = attend(q, k, v, g, bias_mat[...], live)
            score_sum[...] += grads[3]
            for a in range(3):
                back[a, :, slot_rows, :] = grads[a].reshape(FRAMES, ROWS, HEAD)

        folded = jnp.sum(score_sum[...].reshape(FRAMES, ROWS, side), axis=1)
        slots = lax.broadcasted_iota(jnp.int32, (FRAMES, 1), 0)
        distance = frame_of(slots) - query_frame + (FRAMES - 1)

        @pl.loop(0, 2 * FRAMES - 1)
        def _(d):
            bins[pl.ds(d, 1), :] = jnp.sum(
                jnp.where(distance == d, folded, 0.0), axis=0, keepdims=True
            )

        halves = bins[:, :HEAD] + bins[:, HEAD:]
        wide = jnp.concatenate([halves, jnp.zeros((HEAD - 32, HEAD), F32)], axis=0)
        line = jnp.sum(wide.T, axis=0, keepdims=True)
        rows_at = lax.broadcasted_iota(jnp.int32, (8, 1), 0)
        parts[0] += jnp.where(rows_at == head - 3 * y, line, 0.0)

    def home(c, arrays=(0, 1, 2)):
        first, n = CHUNKS[c]
        head, tile = unit_of(me, first)
        extra = n - 6

        def send(slot, size, at, sem):
            rows = pl.ds(slot * ROWS, size * ROWS)
            for a in arrays:
                pltpu.make_async_copy(
                    back.at[a, 0, rows],
                    temporal_out[a].at[tile_rows(at, size), head_cols(head)],
                    home_own.at[sem],
                ).start()
            for a in arrays:
                for step in STEPS:
                    from_slot = ((4 - along_y(step)) % 4) * 4 + step[1] * 2 + step[2]
                    pltpu.make_async_remote_copy(
                        src_ref=back.at[a, from_slot, rows],
                        dst_ref=temporal_out[a].at[tile_rows(at, size), head_cols(head)],
                        send_sem=home_sem.at[sem],
                        recv_sem=home_recv.at[sem],
                        device_id={"seq": peer(step)},
                        device_id_type=MESH,
                    ).start()

        send(first + extra, 6, tile + extra, 0)
        if extra:

            @pl.when(role != 3)
            def _():
                send(first, 1, tile, 1)

    spatial(0, 4)
    temporal(0)
    home(0)
    spatial(4, GROUPS)
    temporal(1)
    home(1, (0,))
    temporal(2)

    pair_copy = pltpu.make_async_remote_copy(
        src_ref=parts.at[0],
        dst_ref=parts.at[1],
        send_sem=sum_send.at[0],
        recv_sem=sum_recv.at[0],
        device_id={"dp": pair},
        device_id_type=MESH,
    )
    pair_copy.start()
    home(1, (1,))
    pair_copy.wait()
    by_x[my_x] = parts[0] + parts[1]
    for other in across:
        pltpu.make_async_remote_copy(
            src_ref=by_x.at[my_x],
            dst_ref=by_x.at[my_x],
            send_sem=sum_send.at[1],
            recv_sem=sum_recv.at[1],
            device_id={"dp": other},
            device_id_type=MESH,
        ).start()
    home(1, (2,))
    three = by_x.at[pl.ds(0, 3)]
    pltpu.make_async_copy(three, three, sum_recv.at[1]).wait()
    pltpu.make_async_copy(three, three, sum_send.at[1]).wait()
    sums[0] = (by_x[0] + by_x[1]) + (by_x[2] + by_x[3])
    for step in STEPS:
        pltpu.make_async_remote_copy(
            src_ref=sums.at[0],
            dst_ref=sums.at[slot_of(step)],
            send_sem=sum_send.at[2],
            recv_sem=sum_recv.at[2],
            device_id={"seq": peer(step)},
            device_id_type=MESH,
        ).start()
    home(2)
    others = sums.at[pl.ds(1, FRAMES - 1)]
    pltpu.make_async_copy(others, others, sum_recv.at[2]).wait()
    pltpu.make_async_copy(others, others, sum_send.at[2]).wait()
    for dy in range(4):
        table[(y + 4 - dy) % 4] = (sums[4 * dy] + sums[4 * dy + 1]) + (
            sums[4 * dy + 2] + sums[4 * dy + 3]
        )

    def wait_all(ref, sem):
        pltpu.make_async_copy(ref, ref, sem).wait()

    common = pl.ds(0, 18 * ROWS)
    peers = pl.ds(1, FRAMES - 1)
    wait_all(recv.at[:, peers, common], out_sem.at[0])
    wait_all(back.at[:, 0, common], home_own.at[0])
    wait_all(back.at[:, peers, common], home_sem.at[0])
    wait_all(back.at[:, peers, common], home_recv.at[0])

    one = pl.ds(0, ROWS)

    @pl.when(role != 3)
    def _():
        wait_all(recv.at[:, pl.ds(0, 11), one], out_sem.at[1])
        wait_all(back.at[:, 0, one], home_own.at[1])
        wait_all(back.at[:, peers, one], home_sem.at[1])
        wait_all(back.at[:, pl.ds(0, 11), one], home_recv.at[1])

    @pl.when(role == 3)
    def _():
        wait_all(recv.at[:, pl.ds(0, 12), one], out_sem.at[1])
        wait_all(back.at[:, pl.ds(0, 12), one], home_recv.at[1])


def store_kernel(*refs):
    copies = [
        pltpu.make_async_copy(made, out, refs[14].at[i])
        for i, (made, out) in enumerate(zip(refs[:6], refs[7:13]))
    ]
    for copy in copies:
        copy.start()
    for row in range(4):
        refs[13][pl.ds(3 * row, 3), :] = refs[6][row, :3, : 2 * FRAMES - 1]
    for copy in copies:
        copy.wait()


def per_device(
    spatial_queries,
    spatial_keys,
    spatial_values,
    spatial_cotangent,
    temporal_queries,
    temporal_keys,
    temporal_values,
    temporal_cotangent,
    frame_bias,
    frame_count,
    grid_height,
    grid_width,
):
    hbm = pl.BlockSpec(memory_space=pl.ANY)
    vmem = pl.BlockSpec(memory_space=pltpu.VMEM)
    dma = pltpu.SemaphoreType.DMA
    spatial_shape = pltpu.VMEM((PATCH, SP_HEADS * HEAD), BF16)
    temporal_shape = pltpu.VMEM((PATCH, TM_HEADS * HEAD), BF16)
    side = FRAMES * ROWS
    outs = pl.pallas_call(
        kernel,
        out_shape=(spatial_shape,) * 3
        + (temporal_shape,) * 3
        + (pltpu.VMEM((4, 8, HEAD), F32),),
        in_specs=[hbm] * 12,
        out_specs=(vmem,) * 7,
        scratch_shapes=[
            pltpu.VMEM((4, QPAD, SP_HEADS * HEAD), BF16),
            pltpu.VMEM((4, FRAMES, SLOTS * ROWS, HEAD), BF16),
            pltpu.VMEM((3, FRAMES, SLOTS * ROWS, HEAD), BF16),
            pltpu.VMEM((side, side), F32),
            pltpu.VMEM((side, side), F32),
            pltpu.VMEM((32, side), F32),
            pltpu.VMEM((2, 8, HEAD), F32),
            pltpu.VMEM((4, 8, HEAD), F32),
            pltpu.VMEM((FRAMES, 8, HEAD), F32),
            pltpu.VMEM((TM_HEADS, 2 * FRAMES - 1), F32),
            pltpu.SMEM((1,), jnp.int32),
            pltpu.SMEM((1,), jnp.int32),
            pltpu.SMEM((1,), jnp.int32),
            dma((4,)),
            dma((GROUPS,)),
            dma((2,)),
            dma((4,)),
            dma((3,)),
            dma((2,)),
            dma((2,)),
            dma((2,)),
            dma((3,)),
            dma((3,)),
        ],
        compiler_params=pltpu.CompilerParams(
            collective_id=0, has_side_effects=True, vmem_limit_bytes=VMEM_LIMIT
        ),
        cost_estimate=pl.CostEstimate(
            flops=8_000_000_000, bytes_accessed=26_000_000, transcendentals=6_000_000
        ),
    )(
        spatial_queries[0, 0],
        spatial_keys[0, 0],
        spatial_values[0, 0],
        spatial_cotangent[0, 0],
        temporal_queries[0, 0],
        temporal_keys[0, 0],
        temporal_values[0, 0],
        temporal_cotangent[0, 0],
        frame_bias,
        frame_count,
        grid_height,
        grid_width,
    )
    stored = pl.pallas_call(
        store_kernel,
        out_shape=tuple(
            jax.ShapeDtypeStruct((PATCH, heads * HEAD), BF16)
            for heads in (SP_HEADS,) * 3 + (TM_HEADS,) * 3
        )
        + (jax.ShapeDtypeStruct((TM_HEADS, 2 * FRAMES - 1), F32),),
        in_specs=[vmem] * 7,
        out_specs=(hbm,) * 6 + (vmem,),
        scratch_shapes=[dma((6,))],
        compiler_params=pltpu.CompilerParams(vmem_limit_bytes=1 << 20),
        cost_estimate=pl.CostEstimate(flops=0, bytes_accessed=11_000_000, transcendentals=0),
    )(*outs)
    return tuple(o[None, None] for o in stored[:6]) + (stored[6],)


def solution(mesh):
    split = P("dp", "seq", None, None)
    in_specs = (split,) * 8 + (P(),) + (P("dp"),) * 3
    out_specs = (split,) * 6 + (P(),)
    return jax.shard_map(
        per_device, mesh=mesh, in_specs=in_specs, out_specs=out_specs, check_vma=False
    )
```
